32 devices in a mesh: parts: 2 (over x), expert: 16 (over z, y, core).
Axes of the slice: x: 2, y: 2, z: 4, core: 2. Of those that a mesh axis runs over, the one named last changes fastest.
Arguments:
- tokens: bfloat16 [256, 4096], P(('parts', 'expert')), parts along dimension 0, may hold values from -6 to 6
- assignments: int32 [256, 8], P(('parts', 'expert')), parts along dimension 0, may hold values from 0 to 3, as said below
- router_gates: float32 [256, 8], P(('parts', 'expert')), parts along dimension 0, may hold values from 0.05 to 0.5
- replica_plan: int32 [4], replicated, may hold values from 0 to 1, as said below
- expert_bias: float32 [2, 4096], replicated, may hold values from -3 to 3
- gate_weight: bfloat16 [16, 4096, 384], P('expert'), may hold values from -0.09375 to 0.09375
- up_weight: bfloat16 [16, 4096, 384], P('expert'), may hold values from -0.09375 to 0.09375
- down_weight: bfloat16 [16, 4096, 384], P('expert'), may hold values from -0.15625 to 0.15625
Outputs:
- expert_mix: bfloat16 [256, 4096], P(('parts', 'expert')), parts along dimension 0
The draws below stay inside these ranges and needn't reach their ends.
There are 2 independent parts, one for each index of `parts`. The reference program is written for one: setup_inputs(seed, part) draws one part's arguments, and reference() takes and returns one part's arrays. A program takes and returns all parts, laid end to end along the dimension named above; an argument that names none is the same for every part. Nothing has to cross between parts.
Inputs may be any that keep to these rules, and one draw needn't show every extreme that they name: `assignments`: in each aligned block of 8 tokens, no replica is named by more than 40 of the block's entries, and some replica is named exactly 40 times in every block. `replica_plan`: every expert is served by at least one replica.
All inputs are finite; a program needn't handle non-finite values.
Results may differ from the reference program's by a relative error of at most 0.0054.
Values may be sent and summed in bfloat16 or wider, within the bound.
A program may use at most 128 MiB of HBM per device.

```python
import math
import jax
import jax.numpy as jnp
from jax import lax

D = 4096
FF = 1536
TOPK = 8
SPLIT = 4
TOK_DEV = 8
TOKENS = 128
EXPERTS = 2
REPLICAS = 4
CAP = 40
N_EXPERT = 16


def draw_assignments(key, part):
    key = jax.random.fold_in(key, 11)
    blocks = TOKENS // TOK_DEV
    pair_count = TOK_DEV * TOPK
    hot_key, block_key = jax.random.split(key)
    hottest = jax.random.randint(hot_key, (), 0, REPLICAS)
    label_pool = jnp.arange((REPLICAS - 1) * CAP, dtype=jnp.int32) // CAP
    label_pool = label_pool + (label_pool >= hottest).astype(jnp.int32)

    def one_block(block_entry):
        first_key, second_key = jax.random.split(block_entry)
        rest_labels = jax.random.permutation(first_key, label_pool)[:pair_count - CAP]
        labels = jnp.concatenate([jnp.full((CAP,), hottest, jnp.int32), rest_labels.astype(jnp.int32)])
        return jax.random.permutation(second_key, labels)
    block_keys = jax.random.split(block_key, blocks)
    return jax.vmap(one_block)(block_keys).reshape(TOKENS, TOPK).astype(jnp.int32)


def draw_replica_plan(key, part):
    key = jax.random.fold_in(key, 23)
    key_list = jax.random.split(key, 3)
    extra_copies = jax.random.randint(key_list[0], (REPLICAS - EXPERTS,), 0, EXPERTS)
    plan_all = jnp.concatenate([jax.random.permutation(key_list[1], EXPERTS).astype(jnp.int32), extra_copies.astype(jnp.int32)])
    return jax.random.permutation(key_list[2], plan_all).astype(jnp.int32)


def levels(own_key, dims, pieces, least, high):
    loudness, own = 1.0, jax.random.fold_in(own_key, 6)
    for axis_at, shards_of in pieces:
        heights = jnp.exp(jax.random.uniform(jax.random.fold_in(own, axis_at), (shards_of,), jnp.float32, least / len(pieces), high / len(pieces)))
        loudness = loudness * jnp.repeat(heights, dims[axis_at] // shards_of).reshape([-1 if axis == axis_at else 1 for axis in range(len(dims))])
    return loudness


def gaussian(stream_key, dims, width, most, pieces=(), kind=jnp.bfloat16):
    values = jax.random.normal(stream_key, dims, jnp.float32) * width
    if len(pieces) > 0:
        values = levels(stream_key, dims, pieces, -0.22, 0.18) * values
    return jnp.clip(values, min=-most, max=most).astype(kind)


def setup_inputs(seed: int = 0, part: int = 0) -> dict:
    keys = jax.random.split(jax.random.key(seed), 9)
    part_keys = jax.random.split(jax.random.fold_in(keys[8], part), 9)
    tokens = gaussian(part_keys[0], (TOKENS, D), 1.0, 6.0, ((0, 16),))
    assignments = draw_assignments(jax.random.fold_in(jax.random.fold_in(keys[8], part), 71), part)
    router_gates = jnp.clip(jnp.exp(math.log(0.5) - 2.3025851 * jax.random.uniform(part_keys[2], (TOKENS, TOPK), jnp.float32) ** levels(part_keys[2], (TOKENS, TOPK), ((0, 16),), -0.2, 0.2)), 0.05, 0.5)
    replica_plan = draw_replica_plan(jax.random.fold_in(keys[8], 71), part)
    expert_bias = gaussian(keys[4], (EXPERTS, D), 0.5, 3.0, (), jnp.float32)
    gate_weight = gaussian(keys[5], (N_EXPERT, D, FF // SPLIT), D ** -0.5, 0.09375, ((0, 16),))
    up_weight = gaussian(keys[6], (N_EXPERT, D, FF // SPLIT), D ** -0.5, 0.09375, ((0, 16),))
    down_weight = gaussian(keys[7], (N_EXPERT, D, FF // SPLIT), FF ** -0.5, 0.15625, ((0, 16),))
    return dict(tokens=tokens, assignments=assignments, router_gates=router_gates, replica_plan=replica_plan, expert_bias=expert_bias, gate_weight=gate_weight, up_weight=up_weight, down_weight=down_weight)


def reference(tokens, assignments, router_gates, replica_plan, expert_bias, gate_weight, up_weight, down_weight):
    pair_replica = assignments.reshape(-1)
    pair_gate = router_gates.reshape(-1)
    pair_token = jnp.arange(TOKENS * TOPK, dtype=jnp.int32) // TOPK
    row_limit = N_EXPERT * CAP

    def one_replica(running, replica):
        named = pair_replica == replica
        found = jnp.nonzero(named, size=row_limit, fill_value=0)[0]
        count = jnp.sum(named.astype(jnp.int32))
        valid = jnp.arange(row_limit, dtype=jnp.int32) < count
        token_index = pair_token[found]
        rows = tokens[token_index]
        summed = jnp.zeros((row_limit, D), jnp.float32)
        for part_index in range(SPLIT):
            host = replica * SPLIT + part_index
            gate_pre = jnp.dot(rows, gate_weight[host], preferred_element_type=jnp.float32)
            up_pre = jnp.dot(rows, up_weight[host], preferred_element_type=jnp.float32)
            hidden = (jax.nn.silu(gate_pre) * up_pre).astype(jnp.bfloat16)
            partial_value = jnp.dot(hidden, down_weight[host].T, preferred_element_type=jnp.float32)
            rounded = lax.optimization_barrier(partial_value.astype(jnp.bfloat16))
            summed = summed + rounded.astype(jnp.float32)
        expert = replica_plan[replica]
        scale = jnp.where(valid, pair_gate[found], jnp.zeros_like(pair_gate[found]))
        contribution = scale[:, None] * (summed + expert_bias[expert][None, :])
        return running.at[token_index].add(contribution), None

    start = jnp.zeros((TOKENS, D), jnp.float32)
    running, _ = lax.scan(one_replica, start, jnp.arange(REPLICAS, dtype=jnp.int32))
    return running.astype(jnp.bfloat16)
```

```python
import functools

import jax
import jax.numpy as jnp
from jax import lax
from jax.experimental import pallas as pl
from jax.experimental.pallas import tpu as pltpu
from jax.sharding import PartitionSpec as P

SPLIT = 4
ROW_BLOCK = 16
IN_CHUNKS = 4
OUT_CHUNKS = 4
MESH = pl.DeviceIdType.MESH


def kernel(
    tokens_ref,
    assign_ref,
    router_ref,
    plan_ref,
    bias_ref,
    gate_hbm,
    up_hbm,
    down_hbm,
    out_ref,
    xbuf,
    w_in,
    w_down,
    acc,
    hidden,
    own_core,
    send_core,
    recv_core,
    own_y,
    send_y,
    recv_y,
    own_z,
    send_z,
    recv_z,
    own_sem,
    w_in_sem,
    w_down_sem,
    in_z_send,
    in_z_recv,
    in_y_send,
    in_y_recv,
    in_c_send,
    in_c_recv,
    out_c_send,
    out_c_recv,
    out_y_send,
    out_y_recv,
    out_z_send,
    out_z_recv,
):
    n = lax.axis_size("expert")
    reps = n // SPLIT
    me = lax.axis_index("expert")
    rep = me // SPLIT
    core_peer = me + 1 - 2 * (me % 2)
    y_peer = me + 2 - 4 * ((me // 2) % 2)

    def z_peer(k):
        return (me + k * SPLIT) % n

    slots = xbuf.shape[1]
    in_width = xbuf.shape[3]
    out_width = recv_z.shape[3]
    units = hidden.shape[1]
    tok = xbuf.shape[2]
    in_chunks, out_chunks = xbuf.shape[0], recv_z.shape[0]

    def remote(src, dst, send_sem, recv_sem, peer):
        return pltpu.make_async_remote_copy(
            src_ref=src,
            dst_ref=dst,
            send_sem=send_sem,
            recv_sem=recv_sem,
            device_id={"expert": peer},
            device_id_type=MESH,
        )

    def own_copy(c):
        return pltpu.make_async_copy(
            tokens_ref.at[:, pl.ds(c * in_width, in_width)], xbuf.at[c, 0], own_sem.at[c]
        )

    def w_copies(c):
        rows = pl.ds(c * in_width, in_width)
        return [
            pltpu.make_async_copy(
                gate_hbm.at[0, rows, :], w_in.at[rows, pl.ds(0, units)], w_in_sem.at[c, 0]
            ),
            pltpu.make_async_copy(
                up_hbm.at[0, rows, :], w_in.at[rows, pl.ds(units, units)], w_in_sem.at[c, 1]
            ),
        ]

    def down_copy(c):
        rows = pl.ds(c * out_width, out_width)
        return pltpu.make_async_copy(down_hbm.at[0, rows, :], w_down.at[rows, :], w_down_sem.at[c])

    for c in range(in_chunks):
        own_copy(c).start()
    for c in range(in_chunks):
        for copy in w_copies(c):
            copy.start()
    for c in range(out_chunks):
        down_copy(c).start()

    barrier = pltpu.get_barrier_semaphore()
    peers = [core_peer, y_peer] + [z_peer(k) for k in range(1, reps)]
    for peer in peers:
        pl.semaphore_signal(barrier, inc=1, device_id={"expert": peer}, device_id_type=MESH)
    pl.semaphore_wait(barrier, len(peers))

    def in_z(c, k):
        return remote(
            xbuf.at[c, 0],
            xbuf.at[c, reps - k],
            in_z_send.at[c, k],
            in_z_recv.at[c, reps - k],
            z_peer(k),
        )

    def in_y(c, k):
        return remote(
            xbuf.at[c, k], xbuf.at[c, reps + k], in_y_send.at[c, k], in_y_recv.at[c, k], y_peer
        )

    def in_c(c, k):
        return remote(
            xbuf.at[c, k],
            xbuf.at[c, 2 * reps + k],
            in_c_send.at[c, k],
            in_c_recv.at[c, k],
            core_peer,
        )

    order = sorted(range(1, reps), key=lambda k: min(k, reps - k))
    for c in range(in_chunks):
        own_copy(c).wait()
        for k in order:
            in_z(c, k).start()
        in_y(c, 0).start()
        in_c(c, 0).start()

    assign = assign_ref[...]
    router = router_ref[...]
    slot_expert = jnp.zeros_like(assign)
    for r in range(reps):
        slot_expert = jnp.where(assign == r, plan_ref[r], slot_expert)

    def replica_weight(k):
        return jnp.sum(
            jnp.where(assign == (rep + k) % reps, router, 0.0), axis=1, keepdims=True
        )

    def expert_weight(e):
        return jnp.sum(jnp.where(slot_expert == e, router, 0.0), axis=1, keepdims=True)

    def pass_on(c):
        for k in order:
            in_z(c, reps - k).wait_recv()
            in_y(c, k).start()
            in_c(c, k).start()
        for k in [0] + order:
            in_y(c, k).wait_recv()
            in_c(c, reps + k).start()

    row_blocks = slots // ROW_BLOCK
    rows_step = ROW_BLOCK * tok

    def multiply_in(c):
        for copy in w_copies(c):
            copy.wait()
        for k in [0] + order:
            in_c(c, k).wait_recv()
        for k in [0] + order:
            in_c(c, reps + k).wait_recv()

        def step(i, carry):
            x = xbuf[c, pl.ds(i * ROW_BLOCK, ROW_BLOCK)]
            x = x.astype(jnp.float32).reshape(rows_step, in_width).astype(jnp.bfloat16)
            w = w_in[pl.ds(c * in_width, in_width), :]
            product = jnp.dot(x, w, preferred_element_type=jnp.float32)
            if c == 0:
                acc[i] = product
            else:
                acc[i] = acc[i] + product
            return carry

        if row_blocks == 1:
            step(0, 0)
        else:
            lax.fori_loop(0, row_blocks, step, 0)

    for c in range(in_chunks):
        pass_on(c)
        if c > 0:
            multiply_in(c - 1)
    multiply_in(in_chunks - 1)

    def activate(i, carry):
        both = acc[i]
        gate = both[:, :units]
        up = both[:, units:]
        value = (gate / (1.0 + jnp.exp(-gate)) * up).astype(jnp.bfloat16)
        hidden[pl.ds(pl.multiple_of(i * rows_step, rows_step), rows_step), :] = value
        return carry

    if row_blocks == 1:
        activate(0, 0)
    else:
        lax.fori_loop(0, row_blocks, activate, 0)

    def out_c(c):
        return remote(
            send_core.at[c], recv_core.at[c], out_c_send.at[c], out_c_recv.at[c], core_peer
        )

    def out_y(c):
        return remote(send_y.at[c], recv_y.at[c], out_y_send.at[c], out_y_recv.at[c], y_peer)

    def out_z(c, k):
        return remote(
            send_z.at[c, k],
            recv_z.at[c, reps - k],
            out_z_send.at[c, k],
            out_z_recv.at[c, reps - k],
            z_peer(k),
        )

    half = slots // 2

    def multiply_out(c):
        down_copy(c).wait()
        w = w_down[pl.ds(c * out_width, out_width), :]

        def product(first_slot, count):
            h = hidden[pl.ds(pl.multiple_of(first_slot * tok, 16), count * tok), :]
            p = lax.dot_general(
                h, w, (((1,), (1,)), ((), ())), preferred_element_type=jnp.float32
            )
            return p.reshape(count, tok, out_width)

        if half < ROW_BLOCK:
            p = product(0, slots)
            send_core[c] = p[half:].astype(jnp.bfloat16)
            out_c(c).start()
            own_core[c] = p[:half]
        else:
            def step(i, carry):
                at = pl.ds(i * ROW_BLOCK, ROW_BLOCK)
                send_core[c, at] = product(half + i * ROW_BLOCK, ROW_BLOCK).astype(jnp.bfloat16)
                own_core[c, at] = product(i * ROW_BLOCK, ROW_BLOCK)
                return carry

            lax.fori_loop(0, half // ROW_BLOCK, step, 0)
            out_c(c).start()

    def sum_cores(c):
        out_c(c).wait_recv()
        send_y[c] = (
            own_core[c, pl.ds(reps, reps)]
            + recv_core[c, pl.ds(reps, reps)].astype(jnp.float32)
        ).astype(jnp.bfloat16)
        out_y(c).start()
        own_y[c] = own_core[c, pl.ds(0, reps)] + recv_core[c, pl.ds(0, reps)].astype(jnp.float32)

    def sum_y(c):
        out_y(c).wait_recv()
        for k in order:
            send_z[c, k] = (own_y[c, k] + recv_y[c, k].astype(jnp.float32)).astype(jnp.bfloat16)
            out_z(c, k).start()
        own_z[c] = own_y[c, 0] + recv_y[c, 0].astype(jnp.float32)

    def finish(c):
        columns = pl.ds(c * out_width, out_width)
        total = replica_weight(0) * own_z[c]
        for e in range(bias_ref.shape[0]):
            total = total + expert_weight(e) * bias_ref[pl.ds(e, 1), columns]
        for k in order:
            out_z(c, reps - k).wait_recv()
            total = total + replica_weight(k) * recv_z[c, k].astype(jnp.float32)
        out_ref[:, columns] = total.astype(jnp.bfloat16)

    for s in range(out_chunks + 3):
        if s < out_chunks:
            multiply_out(s)
        if 0 <= s - 1 < out_chunks:
            sum_cores(s - 1)
        if 0 <= s - 2 < out_chunks:
            sum_y(s - 2)
        if 0 <= s - 3 < out_chunks:
            finish(s - 3)

    for c in range(in_chunks):
        for k in range(1, reps):
            in_z(c, k).wait_send()
        for k in range(reps):
            in_y(c, k).wait_send()
        for k in range(2 * reps):
            in_c(c, k).wait_send()
    for c in range(out_chunks):
        out_c(c).wait_send()
        out_y(c).wait_send()
        for k in range(1, reps):
            out_z(c, k).wait_send()


def local(
    tokens,
    assignments,
    router_gates,
    replica_plan,
    expert_bias,
    gate_weight,
    up_weight,
    down_weight,
):
    n = lax.axis_size("expert")
    tok, width = tokens.shape
    units = gate_weight.shape[2]
    reps = n // SPLIT
    ci, co = IN_CHUNKS, OUT_CHUNKS
    wi, wo = width // ci, width // co
    half = n // 2
    row_blocks = n // ROW_BLOCK
    vmem = pl.BlockSpec(memory_space=pltpu.VMEM)
    smem = pl.BlockSpec(memory_space=pltpu.SMEM)
    hbm = pl.BlockSpec(memory_space=pltpu.HBM)
    dma = pltpu.SemaphoreType.DMA
    bf16, f32 = jnp.bfloat16, jnp.float32
    return pl.pallas_call(
        kernel,
        out_shape=jax.ShapeDtypeStruct((tok, width), bf16),
        in_specs=[hbm, vmem, vmem, smem, vmem, hbm, hbm, hbm],
        out_specs=vmem,
        scratch_shapes=[
            pltpu.VMEM((ci, n, tok, wi), bf16),
            pltpu.VMEM((width, 2 * units), bf16),
            pltpu.VMEM((width, units), bf16),
            pltpu.VMEM((row_blocks, ROW_BLOCK * tok, 2 * units), f32),
            pltpu.VMEM((n * tok, units), bf16),
            pltpu.VMEM((co, half, tok, wo), f32),
            pltpu.VMEM((co, half, tok, wo), bf16),
            pltpu.VMEM((co, half, tok, wo), bf16),
            pltpu.VMEM((co, reps, tok, wo), f32),
            pltpu.VMEM((co, reps, tok, wo), bf16),
            pltpu.VMEM((co, reps, tok, wo), bf16),
            pltpu.VMEM((co, tok, wo), f32),
            pltpu.VMEM((co, reps, tok, wo), bf16),
            pltpu.VMEM((co, reps, tok, wo), bf16),
            dma((ci,)),
            dma((ci, 2)),
            dma((co,)),
            dma((ci, reps)),
            dma((ci, reps)),
            dma((ci, reps)),
            dma((ci, reps)),
            dma((ci, 2 * reps)),
            dma((ci, 2 * reps)),
            dma((co,)),
            dma((co,)),
            dma((co,)),
            dma((co,)),
            dma((co, reps)),
            dma((co, reps)),
        ],
        compiler_params=pltpu.CompilerParams(
            collective_id=0, has_side_effects=True, vmem_limit_bytes=60 * 1024 * 1024
        ),
        cost_estimate=pl.CostEstimate(
            flops=6 * n * tok * width * units,
            bytes_accessed=6 * width * units,
            transcendentals=n * tok * units,
        ),
        name="routed_experts",
    )(
        tokens,
        assignments,
        router_gates,
        replica_plan,
        expert_bias,
        gate_weight,
        up_weight,
        down_weight,
    )


def solution(mesh):
    in_specs = (
        P(("parts", "expert"), None),
        P(("parts", "expert"), None),
        P(("parts", "expert"), None),
        P(),
        P(),
        P("expert", None, None),
        P("expert", None, None),
        P("expert", None, None),
    )
    out_specs = P(("parts", "expert"), None)
    return jax.shard_map(local, mesh=mesh, in_specs=in_specs, out_specs=out_specs, check_vma=False)
```

```python
import functools

import jax
import jax.numpy as jnp
from jax import lax
from jax.experimental import pallas as pl
from jax.experimental.pallas import tpu as pltpu
from jax.sharding import PartitionSpec as P

SPLIT = 4
ROW_BLOCK = 16
IN_CHUNKS = 2
OUT_CHUNKS = 4
MESH = pl.DeviceIdType.MESH


def kernel(
    tokens_ref,
    assign_hbm,
    router_hbm,
    plan_hbm,
    bias_hbm,
    gate_hbm,
    up_hbm,
    down_hbm,
    out_hbm,
    assign_ref,
    router_ref,
    plan_ref,
    bias_ref,
    out_ref,
    xbuf,
    w_in,
    w_down,
    acc,
    hidden,
    own_core,
    send_core,
    recv_core,
    own_y,
    send_y,
    recv_y,
    own_z,
    send_z,
    recv_z,
    small_sem,
    out_sem,
    own_sem,
    w_in_sem,
    w_down_sem,
    in_z_send,
    in_z_recv,
    in_y_send,
    in_y_recv,
    in_c_send,
    in_c_recv,
    out_c_send,
    out_c_recv,
    out_y_send,
    out_y_recv,
    out_z_send,
    out_z_recv,
):
    n = lax.axis_size("expert")
    reps = n // SPLIT
    me = lax.axis_index("expert")
    rep = me // SPLIT
    core_peer = me + 1 - 2 * (me % 2)
    y_peer = me + 2 - 4 * ((me // 2) % 2)

    def z_peer(k):
        return (me + k * SPLIT) % n

    slots = xbuf.shape[1]
    in_width = xbuf.shape[3]
    out_width = recv_z.shape[3]
    units = hidden.shape[1]
    tok = xbuf.shape[2]
    in_chunks, out_chunks = xbuf.shape[0], recv_z.shape[0]

    def remote(src, dst, send_sem, recv_sem, peer):
        return pltpu.make_async_remote_copy(
            src_ref=src,
            dst_ref=dst,
            send_sem=send_sem,
            recv_sem=recv_sem,
            device_id={"expert": peer},
            device_id_type=MESH,
        )

    def own_copy(c):
        return pltpu.make_async_copy(
            tokens_ref.at[:, pl.ds(c * in_width, in_width)], xbuf.at[c, 0], own_sem.at[c]
        )

    def w_copies(c):
        rows = pl.ds(c * in_width, in_width)
        return [
            pltpu.make_async_copy(
                gate_hbm.at[0, rows, :], w_in.at[rows, pl.ds(0, units)], w_in_sem.at[c, 0]
            ),
            pltpu.make_async_copy(
                up_hbm.at[0, rows, :], w_in.at[rows, pl.ds(units, units)], w_in_sem.at[c, 1]
            ),
        ]

    def down_copy(c):
        rows = pl.ds(c * out_width, out_width)
        return pltpu.make_async_copy(down_hbm.at[0, rows, :], w_down.at[rows, :], w_down_sem.at[c])

    for c in range(in_chunks):
        own_copy(c).start()
    for c in range(in_chunks):
        for copy in w_copies(c):
            copy.start()
    for c in range(out_chunks):
        down_copy(c).start()
    small_copies = [
        pltpu.make_async_copy(src, dst, small_sem.at[i])
        for i, (src, dst) in enumerate(
            [
                (assign_hbm, assign_ref),
                (router_hbm, router_ref),
                (plan_hbm, plan_ref),
                (bias_hbm, bias_ref),
            ]
        )
    ]
    for copy in small_copies:
        copy.start()

    barrier = pltpu.get_barrier_semaphore()
    peers = [core_peer, y_peer] + [z_peer(k) for k in range(1, reps)]
    for peer in peers:
        pl.semaphore_signal(barrier, inc=1, device_id={"expert": peer}, device_id_type=MESH)
    pl.semaphore_wait(barrier, len(peers))

    def in_z(c, k):
        return remote(
            xbuf.at[c, 0],
            xbuf.at[c, reps - k],
            in_z_send.at[c, k],
            in_z_recv.at[c, reps - k],
            z_peer(k),
        )

    def in_y(c, k):
        return remote(
            xbuf.at[c, k], xbuf.at[c, reps + k], in_y_send.at[c, k], in_y_recv.at[c, k], y_peer
        )

    def in_c(c, k):
        return remote(
            xbuf.at[c, k],
            xbuf.at[c, 2 * reps + k],
            in_c_send.at[c, k],
            in_c_recv.at[c, k],
            core_peer,
        )

    order = sorted(range(1, reps), key=lambda k: min(k, reps - k))
    for c in range(in_chunks):
        own_copy(c).wait()
        for k in order:
            in_z(c, k).start()
        in_y(c, 0).start()
        in_c(c, 0).start()

    for copy in small_copies:
        copy.wait()

    assign = assign_ref[...]
    router = router_ref[...]
    slot_expert = jnp.zeros_like(assign)
    for r in range(reps):
        slot_expert = jnp.where(assign == r, plan_ref[r], slot_expert)

    def replica_weight(k):
        return jnp.sum(
            jnp.where(assign == (rep + k) % reps, router, 0.0), axis=1, keepdims=True
        )

    def expert_weight(e):
        return jnp.sum(jnp.where(slot_expert == e, router, 0.0), axis=1, keepdims=True)

    def pass_z(c):
        for k in order:
            in_z(c, reps - k).wait_recv()
            in_y(c, k).start()
            in_c(c, k).start()

    def pass_y(c):
        for k in [0] + order:
            in_y(c, k).wait_recv()
            in_c(c, reps + k).start()

    row_blocks = slots // ROW_BLOCK
    rows_step = ROW_BLOCK * tok

    def multiply_in(c):
        for copy in w_copies(c):
            copy.wait()
        for k in [0] + order:
            in_c(c, k).wait_recv()
        for k in [0] + order:
            in_c(c, reps + k).wait_recv()

        def step(i, carry):
            x = xbuf[c, pl.ds(i * ROW_BLOCK, ROW_BLOCK)]
            x = x.astype(jnp.float32).reshape(rows_step, in_width).astype(jnp.bfloat16)
            w = w_in[pl.ds(c * in_width, in_width), :]
            product = jnp.dot(x, w, preferred_element_type=jnp.float32)
            if c == 0:
                acc[i] = product
            else:
                acc[i] = acc[i] + product
            return carry

        if row_blocks == 1:
            step(0, 0)
        else:
            lax.fori_loop(0, row_blocks, step, 0)

    for c in range(in_chunks):
        pass_z(c)
    for c in range(in_chunks):
        pass_y(c)
        if c > 0:
            multiply_in(c - 1)
    multiply_in(in_chunks - 1)

    def activate(i, carry):
        both = acc[i]
        gate = both[:, :units]
        up = both[:, units:]
        value = (gate / (1.0 + jnp.exp(-gate)) * up).astype(jnp.bfloat16)
        hidden[pl.ds(pl.multiple_of(i * rows_step, rows_step), rows_step), :] = value
        return carry

    if row_blocks == 1:
        activate(0, 0)
    else:
        lax.fori_loop(0, row_blocks, activate, 0)

    def out_c(c):
        return remote(
            send_core.at[c], recv_core.at[c], out_c_send.at[c], out_c_recv.at[c], core_peer
        )

    def out_y(c):
        return remote(send_y.at[c], recv_y.at[c], out_y_send.at[c], out_y_recv.at[c], y_peer)

    def out_z(c, k):
        return remote(
            send_z.at[c, k],
            recv_z.at[c, reps - k],
            out_z_send.at[c, k],
            out_z_recv.at[c, reps - k],
            z_peer(k),
        )

    def out_copy(c):
        columns = pl.ds(c * out_width, out_width)
        return pltpu.make_async_copy(out_ref.at[:, columns], out_hbm.at[:, columns], out_sem.at[c])

    half = slots // 2

    def multiply_out(c):
        down_copy(c).wait()
        w = w_down[pl.ds(c * out_width, out_width), :]

        def product(first_slot, count):
            h = hidden[pl.ds(pl.multiple_of(first_slot * tok, 16), count * tok), :]
            p = lax.dot_general(
                h, w, (((1,), (1,)), ((), ())), preferred_element_type=jnp.float32
            )
            return p.reshape(count, tok, out_width)

        if half < ROW_BLOCK:
            p = product(0, slots)
            send_core[c] = p[half:].astype(jnp.bfloat16)
            out_c(c).start()
            own_core[c] = p[:half]
        else:
            def step(i, carry):
                at = pl.ds(i * ROW_BLOCK, ROW_BLOCK)
                send_core[c, at] = product(half + i * ROW_BLOCK, ROW_BLOCK).astype(jnp.bfloat16)
                own_core[c, at] = product(i * ROW_BLOCK, ROW_BLOCK)
                return carry

            lax.fori_loop(0, half // ROW_BLOCK, step, 0)
            out_c(c).start()

    def sum_cores(c):
        out_c(c).wait_recv()
        send_y[c] = (
            own_core[c, pl.ds(reps, reps)]
            + recv_core[c, pl.ds(reps, reps)].astype(jnp.float32)
        ).astype(jnp.bfloat16)
        out_y(c).start()
        own_y[c] = own_core[c, pl.ds(0, reps)] + recv_core[c, pl.ds(0, reps)].astype(jnp.float32)

    def sum_y(c):
        out_y(c).wait_recv()
        for k in order:
            send_z[c, k] = (own_y[c, k] + recv_y[c, k].astype(jnp.float32)).astype(jnp.bfloat16)
            out_z(c, k).start()
        own_z[c] = own_y[c, 0] + recv_y[c, 0].astype(jnp.float32)

    def finish(c):
        columns = pl.ds(c * out_width, out_width)
        total = replica_weight(0) * own_z[c]
        for e in range(bias_ref.shape[0]):
            total = total + expert_weight(e) * bias_ref[pl.ds(e, 1), columns]
        for k in order:
            out_z(c, reps - k).wait_recv()
            total = total + replica_weight(k) * recv_z[c, k].astype(jnp.float32)
        out_ref[:, columns] = total.astype(jnp.bfloat16)
        out_copy(c).start()

    for c in range(out_chunks):
        multiply_out(c)
        if c > 0:
            sum_cores(c - 1)
    sum_cores(out_chunks - 1)
    for c in range(out_chunks):
        sum_y(c)
    for c in range(out_chunks):
        finish(c)

    for c in range(in_chunks):
        for k in range(1, reps):
            in_z(c, k).wait_send()
        for k in range(reps):
            in_y(c, k).wait_send()
        for k in range(2 * reps):
            in_c(c, k).wait_send()
    for c in range(out_chunks):
        out_c(c).wait_send()
        out_y(c).wait_send()
        for k in range(1, reps):
            out_z(c, k).wait_send()
        out_copy(c).wait()


def local(
    tokens,
    assignments,
    router_gates,
    replica_plan,
    expert_bias,
    gate_weight,
    up_weight,
    down_weight,
):
    n = lax.axis_size("expert")
    tok, width = tokens.shape
    units = gate_weight.shape[2]
    reps = n // SPLIT
    ci, co = IN_CHUNKS, OUT_CHUNKS
    wi, wo = width // ci, width // co
    half = n // 2
    row_blocks = n // ROW_BLOCK
    hbm = pl.BlockSpec(memory_space=pltpu.HBM)
    dma = pltpu.SemaphoreType.DMA
    bf16, f32 = jnp.bfloat16, jnp.float32
    return pl.pallas_call(
        kernel,
        out_shape=jax.ShapeDtypeStruct((tok, width), bf16),
        in_specs=[hbm] * 8,
        out_specs=hbm,
        scratch_shapes=[
            pltpu.VMEM(assignments.shape, jnp.int32),
            pltpu.VMEM(router_gates.shape, f32),
            pltpu.SMEM(replica_plan.shape, jnp.int32),
            pltpu.VMEM(expert_bias.shape, f32),
            pltpu.VMEM((tok, width), bf16),
            pltpu.VMEM((ci, n, tok, wi), bf16),
            pltpu.VMEM((width, 2 * units), bf16),
            pltpu.VMEM((width, units), bf16),
            pltpu.VMEM((row_blocks, ROW_BLOCK * tok, 2 * units), f32),
            pltpu.VMEM((n * tok, units), bf16),
            pltpu.VMEM((co, half, tok, wo), f32),
            pltpu.VMEM((co, half, tok, wo), bf16),
            pltpu.VMEM((co, half, tok, wo), bf16),
            pltpu.VMEM((co, reps, tok, wo), f32),
            pltpu.VMEM((co, reps, tok, wo), bf16),
            pltpu.VMEM((co, reps, tok, wo), bf16),
            pltpu.VMEM((co, tok, wo), f32),
            pltpu.VMEM((co, reps, tok, wo), bf16),
            pltpu.VMEM((co, reps, tok, wo), bf16),
            dma((4,)),
            dma((co,)),
            dma((ci,)),
            dma((ci, 2)),
            dma((co,)),
            dma((ci, reps)),
            dma((ci, reps)),
            dma((ci, reps)),
            dma((ci, reps)),
            dma((ci, 2 * reps)),
            dma((ci, 2 * reps)),
            dma((co,)),
            dma((co,)),
            dma((co,)),
            dma((co,)),
            dma((co, reps)),
            dma((co, reps)),
        ],
        compiler_params=pltpu.CompilerParams(
            collective_id=0, has_side_effects=True, vmem_limit_bytes=60 * 1024 * 1024
        ),
        cost_estimate=pl.CostEstimate(
            flops=6 * n * tok * width * units,
            bytes_accessed=6 * width * units,
            transcendentals=n * tok * units,
        ),
        name="routed_experts",
    )(
        tokens,
        assignments,
        router_gates,
        replica_plan,
        expert_bias,
        gate_weight,
        up_weight,
        down_weight,
    )


def solution(mesh):
    in_specs = (
        P(("parts", "expert"), None),
        P(("parts", "expert"), None),
        P(("parts", "expert"), None),
        P(),
        P(),
        P("expert", None, None),
        P("expert", None, None),
        P("expert", None, None),
    )
    out_specs = P(("parts", "expert"), None)
    return jax.shard_map(local, mesh=mesh, in_specs=in_specs, out_specs=out_specs, check_vma=False)
```

```python
import functools

import jax
import jax.numpy as jnp
from jax import lax
from jax.experimental import pallas as pl
from jax.experimental.pallas import tpu as pltpu
from jax.sharding import PartitionSpec as P

SPLIT = 4
ROW_BLOCK = 16
IN_CHUNKS = 2
OUT_CHUNKS = 4
MESH = pl.DeviceIdType.MESH


def kernel(
    tokens_ref,
    assign_hbm,
    router_hbm,
    plan_hbm,
    bias_hbm,
    gate_hbm,
    up_hbm,
    down_hbm,
    out_hbm,
    assign_ref,
    router_ref,
    plan_ref,
    bias_ref,
    out_ref,
    xbuf,
    w_in,
    w_down,
    acc,
    hidden,
    own_core,
    send_core,
    recv_core,
    own_y,
    send_y,
    recv_y,
    own_z,
    send_z,
    recv_z,
    small_sem,
    out_sem,
    own_sem,
    w_in_sem,
    w_down_sem,
    in_z_send,
    in_z_recv,
    in_y_send,
    in_y_recv,
    in_c_send,
    in_c_recv,
    out_c_send,
    out_c_recv,
    out_y_send,
    out_y_recv,
    out_z_send,
    out_z_recv,
):
    n = lax.axis_size("expert")
    reps = n // SPLIT
    me = lax.axis_index("expert")
    rep = me // SPLIT
    core_peer = me + 1 - 2 * (me % 2)
    y_peer = me + 2 - 4 * ((me // 2) % 2)

    def z_peer(k):
        return (me + k * SPLIT) % n

    slots = xbuf.shape[1]
    in_width = xbuf.shape[3]
    out_width = recv_z.shape[3]
    units = hidden.shape[1]
    tok = xbuf.shape[2]
    in_chunks, out_chunks = xbuf.shape[0], recv_z.shape[0]

    def remote(src, dst, send_sem, recv_sem, peer):
        return pltpu.make_async_remote_copy(
            src_ref=src,
            dst_ref=dst,
            send_sem=send_sem,
            recv_sem=recv_sem,
            device_id={"expert": peer},
            device_id_type=MESH,
        )

    def own_copy(c):
        return pltpu.make_async_copy(
            tokens_ref.at[:, pl.ds(c * in_width, in_width)], xbuf.at[c, 0], own_sem.at[c]
        )

    def w_copies(c):
        rows = pl.ds(c * in_width, in_width)
        return [
            pltpu.make_async_copy(
                gate_hbm.at[0, rows, :], w_in.at[rows, pl.ds(0, units)], w_in_sem.at[c, 0]
            ),
            pltpu.make_async_copy(
                up_hbm.at[0, rows, :], w_in.at[rows, pl.ds(units, units)], w_in_sem.at[c, 1]
            ),
        ]

    def down_copy(c):
        rows = pl.ds(c * out_width, out_width)
        return pltpu.make_async_copy(down_hbm.at[0, rows, :], w_down.at[rows, :], w_down_sem.at[c])

    for c in range(in_chunks):
        own_copy(c).start()
    for c in range(in_chunks):
        for copy in w_copies(c):
            copy.start()
    for c in range(out_chunks):
        down_copy(c).start()
    small_copies = [
        pltpu.make_async_copy(src, dst, small_sem.at[i])
        for i, (src, dst) in enumerate(
            [
                (assign_hbm, assign_ref),
                (router_hbm, router_ref),
                (plan_hbm, plan_ref),
                (bias_hbm, bias_ref),
            ]
        )
    ]
    for copy in small_copies:
        copy.start()

    barrier = pltpu.get_barrier_semaphore()
    peers = [core_peer, y_peer] + [z_peer(k) for k in range(1, reps)]
    for peer in peers:
        pl.semaphore_signal(barrier, inc=1, device_id={"expert": peer}, device_id_type=MESH)
    pl.semaphore_wait(barrier, len(peers))

    def in_z(c, k):
        return remote(
            xbuf.at[c, 0],
            xbuf.at[c, reps - k],
            in_z_send.at[c, k],
            in_z_recv.at[c, reps - k],
            z_peer(k),
        )

    def in_y(c, k):
        return remote(
            xbuf.at[c, k], xbuf.at[c, reps + k], in_y_send.at[c, k], in_y_recv.at[c, k], y_peer
        )

    def in_c(c, y):
        return remote(
            xbuf.at[c, pl.ds(y * reps, reps)],
            xbuf.at[c, pl.ds((2 + y) * reps, reps)],
            in_c_send.at[c, y],
            in_c_recv.at[c, y],
            core_peer,
        )

    order = sorted(range(1, reps), key=lambda k: min(k, reps - k))
    for c in range(in_chunks):
        own_copy(c).wait()
        for k in order:
            in_z(c, k).start()
        in_y(c, 0).start()

    for copy in small_copies:
        copy.wait()

    assign = assign_ref[...]
    router = router_ref[...]
    slot_expert = jnp.zeros_like(assign)
    for r in range(reps):
        slot_expert = jnp.where(assign == r, plan_ref[r], slot_expert)

    def replica_weight(k):
        return jnp.sum(
            jnp.where(assign == (rep + k) % reps, router, 0.0), axis=1, keepdims=True
        )

    def expert_weight(e):
        return jnp.sum(jnp.where(slot_expert == e, router, 0.0), axis=1, keepdims=True)

    def pass_z(c):
        for k in order:
            in_z(c, reps - k).wait_recv()
            in_y(c, k).start()
        in_c(c, 0).start()

    def pass_y(c):
        for k in [0] + order:
            in_y(c, k).wait_recv()
        in_c(c, 1).start()

    row_blocks = slots // ROW_BLOCK
    rows_step = ROW_BLOCK * tok

    def multiply_in(c):
        for copy in w_copies(c):
            copy.wait()
        in_c(c, 0).wait_recv()
        in_c(c, 1).wait_recv()

        def step(i, carry):
            x = xbuf[c, pl.ds(i * ROW_BLOCK, ROW_BLOCK)]
            x = x.astype(jnp.float32).reshape(rows_step, in_width).astype(jnp.bfloat16)
            w = w_in[pl.ds(c * in_width, in_width), :]
            product = jnp.dot(x, w, preferred_element_type=jnp.float32)
            if c == 0:
                acc[i] = product
            else:
                acc[i] = acc[i] + product
            return carry

        if row_blocks == 1:
            step(0, 0)
        else:
            lax.fori_loop(0, row_blocks, step, 0)

    for c in range(in_chunks):
        pass_z(c)
    for c in range(in_chunks):
        pass_y(c)
        if c > 0:
            multiply_in(c - 1)
    multiply_in(in_chunks - 1)

    def activate(i, carry):
        both = acc[i]
        gate = both[:, :units]
        up = both[:, units:]
        value = (gate / (1.0 + jnp.exp(-gate)) * up).astype(jnp.bfloat16)
        hidden[pl.ds(pl.multiple_of(i * rows_step, rows_step), rows_step), :] = value
        return carry

    if row_blocks == 1:
        activate(0, 0)
    else:
        lax.fori_loop(0, row_blocks, activate, 0)

    def out_c(c):
        return remote(
            send_core.at[c], recv_core.at[c], out_c_send.at[c], out_c_recv.at[c], core_peer
        )

    def out_y(c):
        return remote(send_y.at[c], recv_y.at[c], out_y_send.at[c], out_y_recv.at[c], y_peer)

    def out_z(c, k):
        return remote(
            send_z.at[c, k],
            recv_z.at[c, reps - k],
            out_z_send.at[c, k],
            out_z_recv.at[c, reps - k],
            z_peer(k),
        )

    def out_copy(c):
        columns = pl.ds(c * out_width, out_width)
        return pltpu.make_async_copy(out_ref.at[:, columns], out_hbm.at[:, columns], out_sem.at[c])

    half = slots // 2

    def multiply_out(c):
        down_copy(c).wait()
        w = w_down[pl.ds(c * out_width, out_width), :]

        def product(first_slot, count):
            h = hidden[pl.ds(pl.multiple_of(first_slot * tok, 16), count * tok), :]
            p = lax.dot_general(
                h, w, (((1,), (1,)), ((), ())), preferred_element_type=jnp.float32
            )
            return p.reshape(count, tok, out_width)

        if half < ROW_BLOCK:
            p = product(0, slots)
            send_core[c] = p[half:].astype(jnp.bfloat16)
            out_c(c).start()
            own_core[c] = p[:half]
        else:
            def step(i, carry):
                at = pl.ds(i * ROW_BLOCK, ROW_BLOCK)
                send_core[c, at] = product(half + i * ROW_BLOCK, ROW_BLOCK).astype(jnp.bfloat16)
                own_core[c, at] = product(i * ROW_BLOCK, ROW_BLOCK)
                return carry

            lax.fori_loop(0, half // ROW_BLOCK, step, 0)
            out_c(c).start()

    def sum_cores(c):
        out_c(c).wait_recv()
        send_y[c] = (
            own_core[c, pl.ds(reps, reps)]
            + recv_core[c, pl.ds(reps, reps)].astype(jnp.float32)
        ).astype(jnp.bfloat16)
        out_y(c).start()
        own_y[c] = own_core[c, pl.ds(0, reps)] + recv_core[c, pl.ds(0, reps)].astype(jnp.float32)

    def sum_y(c):
        out_y(c).wait_recv()
        for k in order:
            send_z[c, k] = (own_y[c, k] + recv_y[c, k].astype(jnp.float32)).astype(jnp.bfloat16)
            out_z(c, k).start()
        own_z[c] = own_y[c, 0] + recv_y[c, 0].astype(jnp.float32)

    def finish(c):
        columns = pl.ds(c * out_width, out_width)
        total = replica_weight(0) * own_z[c]
        for e in range(bias_ref.shape[0]):
            total = total + expert_weight(e) * bias_ref[pl.ds(e, 1), columns]
        for k in order:
            out_z(c, reps - k).wait_recv()
            total = total + replica_weight(k) * recv_z[c, k].astype(jnp.float32)
        out_ref[:, columns] = total.astype(jnp.bfloat16)
        out_copy(c).start()

    for c in range(out_chunks):
        multiply_out(c)
        if c > 0:
            sum_cores(c - 1)
    sum_cores(out_chunks - 1)
    for c in range(out_chunks):
        sum_y(c)
    for c in range(out_chunks):
        finish(c)

    for c in range(in_chunks):
        for k in range(1, reps):
            in_z(c, k).wait_send()
        for k in range(reps):
            in_y(c, k).wait_send()
        in_c(c, 0).wait_send()
        in_c(c, 1).wait_send()
    for c in range(out_chunks):
        out_c(c).wait_send()
        out_y(c).wait_send()
        for k in range(1, reps):
            out_z(c, k).wait_send()
        out_copy(c).wait()


def local(
    tokens,
    assignments,
    router_gates,
    replica_plan,
    expert_bias,
    gate_weight,
    up_weight,
    down_weight,
):
    n = lax.axis_size("expert")
    tok, width = tokens.shape
    units = gate_weight.shape[2]
    reps = n // SPLIT
    ci, co = IN_CHUNKS, OUT_CHUNKS
    wi, wo = width // ci, width // co
    half = n // 2
    row_blocks = n // ROW_BLOCK
    hbm = pl.BlockSpec(memory_space=pltpu.HBM)
    dma = pltpu.SemaphoreType.DMA
    bf16, f32 = jnp.bfloat16, jnp.float32
    return pl.pallas_call(
        kernel,
        out_shape=jax.ShapeDtypeStruct((tok, width), bf16),
        in_specs=[hbm] * 8,
        out_specs=hbm,
        scratch_shapes=[
            pltpu.VMEM(assignments.shape, jnp.int32),
            pltpu.VMEM(router_gates.shape, f32),
            pltpu.SMEM(replica_plan.shape, jnp.int32),
            pltpu.VMEM(expert_bias.shape, f32),
            pltpu.VMEM((tok, width), bf16),
            pltpu.VMEM((ci, n, tok, wi), bf16),
            pltpu.VMEM((width, 2 * units), bf16),
            pltpu.VMEM((width, units), bf16),
            pltpu.VMEM((row_blocks, ROW_BLOCK * tok, 2 * units), f32),
            pltpu.VMEM((n * tok, units), bf16),
            pltpu.VMEM((co, half, tok, wo), f32),
            pltpu.VMEM((co, half, tok, wo), bf16),
            pltpu.VMEM((co, half, tok, wo), bf16),
            pltpu.VMEM((co, reps, tok, wo), f32),
            pltpu.VMEM((co, reps, tok, wo), bf16),
            pltpu.VMEM((co, reps, tok, wo), bf16),
            pltpu.VMEM((co, tok, wo), f32),
            pltpu.VMEM((co, reps, tok, wo), bf16),
            pltpu.VMEM((co, reps, tok, wo), bf16),
            dma((4,)),
            dma((co,)),
            dma((ci,)),
            dma((ci, 2)),
            dma((co,)),
            dma((ci, reps)),
            dma((ci, reps)),
            dma((ci, reps)),
            dma((ci, reps)),
            dma((ci, 2)),
            dma((ci, 2)),
            dma((co,)),
            dma((co,)),
            dma((co,)),
            dma((co,)),
            dma((co, reps)),
            dma((co, reps)),
        ],
        compiler_params=pltpu.CompilerParams(
            collective_id=0, has_side_effects=True, vmem_limit_bytes=60 * 1024 * 1024
        ),
        cost_estimate=pl.CostEstimate(
            flops=6 * n * tok * width * units,
            bytes_accessed=6 * width * units,
            transcendentals=n * tok * units,
        ),
        name="routed_experts",
    )(
        tokens,
        assignments,
        router_gates,
        replica_plan,
        expert_bias,
        gate_weight,
        up_weight,
        down_weight,
    )


def solution(mesh):
    in_specs = (
        P(("parts", "expert"), None),
        P(("parts", "expert"), None),
        P(("parts", "expert"), None),
        P(),
        P(),
        P("expert", None, None),
        P("expert", None, None),
        P("expert", None, None),
    )
    out_specs = P(("parts", "expert"), None)
    return jax.shard_map(local, mesh=mesh, in_specs=in_specs, out_specs=out_specs, check_vma=False)
```
